1024 devices in a mesh: row: 64 (over y_lo, z), col: 16 (over y_hi, x, core).
Axes of the slice: x: 4, y: 8 (y_hi: 2, y_lo: 4; y = y_hi * 4 + y_lo), z: 16, core: 2. Of those that a mesh axis runs over, the one named last changes fastest.
Arguments:
- current_block: float32 [8, 131072], P(None, ('row', 'col'))
- prior_blocks: float32 [32, 131072], P(None, ('row', 'col'))
- diagonal: float32 [131072], P(('row', 'col')), may hold values from 1 to 4
- stored_tiles: float32 [64, 16, 8, 128, 128], P('row', 'col'), may hold values from -0.1875 to 0.1875
- tile_coords: int32 [64, 16, 2, 8], P('row', 'col'), may hold values from 0 to 63, as said below
- tile_counts: int32 [64, 16], P('row', 'col'), may hold values from 2 to 8, as said below
Outputs:
- new_blocks: float32 [16, 131072], P(None, ('row', 'col'))
The draws below stay inside these ranges and needn't reach their ends.
Inputs may be any that keep to these rules, and one draw needn't show every extreme that they name: `tile_counts`: live slots of one device; some device holds 8. `tile_coords`: index 0 lies below 16, index 1 below 64; positions may repeat.
All inputs are finite; a program needn't handle non-finite values.
Results may differ from the reference program's by a relative error of at most 0.0003.
Values sent between devices are 32-bit elements; how exact they have to be, the bound alone decides.
A program may use at most 32 MiB of HBM per device.

```python
import jax
import jax.numpy as jnp
from jax import lax

TILE = 128
K = 8
PRIOR = 4
STEPS = 2
TP = 1
TILES_DEV = 8
N = 131072
N_ROW = 64
N_COL = 16


def shared_block(key):
    return jax.random.truncated_normal(key, -4.0, 4.0, (K, N), jnp.float32)


def draw_current_block(key, part):
    shared = shared_block(key)
    key = jax.random.fold_in(key, 11)
    own_part = jax.random.truncated_normal(key, -4.0, 4.0, (K, N), jnp.float32)
    return 0.6 * shared + 0.8 * own_part


def draw_prior_blocks(key, part):
    shared = shared_block(key)
    key = jax.random.fold_in(key, 12)
    noise_key, weight_key = jax.random.split(key)
    own_part = jax.random.truncated_normal(noise_key, -4.0, 4.0, (PRIOR, K, N), jnp.float32)
    weights = jax.random.uniform(weight_key, (PRIOR, 1, 1), jnp.float32, 0.2, 0.7)
    return (weights * shared[None] + own_part).reshape(PRIOR * K, N)


def draw_tile_coords(key, part):
    key = jax.random.fold_in(key, 13)
    first_key, second_key = jax.random.split(key)
    tile_rows = jax.random.randint(first_key, (N_ROW, N_COL, 1, TILES_DEV), 0, N_COL * TP, jnp.int32)
    tile_cols = jax.random.randint(second_key, (N_ROW, N_COL, 1, TILES_DEV), 0, N_ROW * TP, jnp.int32)
    return jnp.concatenate([tile_rows, tile_cols], axis=2)


def draw_tile_counts(key, part):
    key = jax.random.fold_in(key, 14)
    base_key, heavy_key, spot_key = jax.random.split(key, 3)
    base_counts = jax.random.randint(base_key, (N_ROW * N_COL,), max(1, TILES_DEV // 4), TILES_DEV // 2 + 1, jnp.int32)
    heavy = jax.random.randint(heavy_key, (N_ROW * N_COL,), 0, 8, jnp.int32) == 0
    counts_all = jnp.where(heavy, TILES_DEV, base_counts)
    spot = jax.random.randint(spot_key, (), 0, N_ROW * N_COL, jnp.int32)
    counts_all = counts_all.at[spot].set(TILES_DEV)
    return counts_all.reshape(N_ROW, N_COL)


def steps_of(rng, shape, pieces, smallest, high):
    factor_of = 1.0
    for position, shards_of in pieces:
        heights = jax.random.uniform(jax.random.fold_in(jax.random.fold_in(rng, 6), position), (shards_of,), jnp.float32, smallest / len(pieces), high / len(pieces))
        factor_of = factor_of * jnp.repeat(jnp.exp(heights), shape[position] // shards_of).reshape((-1,) + (1,) * (len(shape) - 1 - position))
    return factor_of


def scatter_about(stream_key, shape, scale, bound, shards=(), kind=jnp.bfloat16):
    level = steps_of(stream_key, shape, shards, -0.22, 0.18) if shards else 1.0
    array = jax.random.normal(stream_key, shape, jnp.float32) * scale * level
    return jnp.minimum(jnp.maximum(array, -bound), bound).astype(kind)


def setup_inputs(seed: int = 0) -> dict:
    key_list = jax.random.split(jax.random.key(seed), 7)
    current_block = draw_current_block(jax.random.fold_in(key_list[6], 71), 0)
    prior_blocks = draw_prior_blocks(jax.random.fold_in(key_list[6], 71), 0)
    diagonal = jnp.clip(1.0 + 3.0 * jax.random.uniform(key_list[2], (N,), jnp.float32) ** steps_of(key_list[2], (N,), ((0, 1024),), -0.2, 0.2), 1.0, 4.0)
    stored_tiles = scatter_about(key_list[3], (N_ROW, N_COL, TILES_DEV, TILE, TILE), (TILE * TILES_DEV) ** -0.5, 0.1875, ((0, 64), (1, 16)), jnp.float32)
    tile_coords = draw_tile_coords(jax.random.fold_in(key_list[6], 71), 0)
    tile_counts = draw_tile_counts(jax.random.fold_in(key_list[6], 71), 0)
    return {"current_block": current_block, "prior_blocks": prior_blocks, "diagonal": diagonal, "stored_tiles": stored_tiles, "tile_coords": tile_coords, "tile_counts": tile_counts}


HIGH = lax.Precision.HIGHEST

def apply_operator(vectors, stored_tiles, tile_coords, tile_counts, diagonal):
    vec_rows = vectors.shape[0]
    tiled_vec = vectors.reshape(vec_rows, N // TILE, TILE)
    device_tiles = stored_tiles.reshape(N_ROW * N_COL, TILES_DEV, TILE, TILE)
    device_where = tile_coords.reshape(N_ROW * N_COL, 2, TILES_DEV)
    device_counts = tile_counts.reshape(N_ROW * N_COL)
    device_ids = jnp.arange(N_ROW * N_COL, dtype=jnp.int32)

    def add_device(totals, device_item):
        device_index, tile_block, tile_where, slot_count = device_item
        row_index = device_index // N_COL
        col_index = device_index % N_COL
        live_slots = (jnp.arange(TILES_DEV, dtype=jnp.int32) < slot_count).astype(jnp.float32)
        tile_rows = (row_index * (N_COL * TP) + tile_where[0]).astype(jnp.int32)
        tile_cols = ((tile_where[1] // TP * N_COL + col_index) * TP + tile_where[1] % TP).astype(jnp.int32)
        row_inputs = tiled_vec[:, tile_rows]
        col_inputs = tiled_vec[:, tile_cols]
        to_rows = jnp.einsum('kti,tji->ktj', col_inputs, tile_block, precision=HIGH) * live_slots[None, :, None]
        to_cols = jnp.einsum('kti,tij->ktj', row_inputs, tile_block, precision=HIGH) * live_slots[None, :, None]
        totals = totals.at[:, tile_rows].add(to_rows)
        totals = totals.at[:, tile_cols].add(to_cols)
        return (totals, None)
    start = jnp.zeros((vec_rows, N // TILE, TILE), jnp.float32)
    totals, _ = lax.scan(add_device, start, (device_ids, device_tiles, device_where, device_counts))
    return totals.reshape(vec_rows, N) + diagonal[None, :] * vectors

def reference(current_block, prior_blocks, diagonal, stored_tiles, tile_coords, tile_counts):
    window = prior_blocks
    current = current_block
    produced = []
    for step_index in range(STEPS):
        image_block = apply_operator(current, stored_tiles, tile_coords, tile_counts, diagonal)
        basis_rows = jnp.concatenate([window, current], axis=0)
        projection = jnp.dot(basis_rows, image_block.T, precision=HIGH) / N
        remainder = image_block - jnp.dot(projection.T, basis_rows, precision=HIGH)
        gram_matrix = jnp.dot(remainder, remainder.T, precision=HIGH) / N
        lower_factor = jnp.linalg.cholesky(gram_matrix)
        fresh = lax.linalg.triangular_solve(lower_factor, remainder, left_side=True, lower=True)
        produced.append(fresh)
        window = jnp.concatenate([window[K:], current], axis=0)
        current = fresh
    return jnp.concatenate(produced, axis=0)
```

```python
import functools

import jax
import jax.numpy as jnp
from jax import lax
from jax.experimental import pallas as pl
from jax.experimental.pallas import tpu as pltpu
from jax.sharding import PartitionSpec as P

MESH = pl.DeviceIdType.MESH
HIGH = lax.Precision.HIGHEST
F32 = jnp.float32
BF16 = jnp.bfloat16

LAYOUT = dict(y_lo=4, z_far=4, y_hi=2, x=4, core=2)
NEAR = 4


class Place:
    def __init__(self, lay):
        self.lay = lay
        self.nz = lay["z_far"] * NEAR
        self.ncol = lay["y_hi"] * lay["x"] * lay["core"]
        self.fold = lay["x"] * lay["core"]
        self.ny = lay["y_lo"] * lay["y_hi"]
        self.r = lax.axis_index("row")
        self.c = lax.axis_index("col")
        self.y = lax.div(self.r, self.nz)
        self.z = lax.rem(self.r, self.nz)
        self.z_far = lax.div(self.z, NEAR)
        self.z_near = lax.rem(self.z, NEAR)
        self.y_hi = lax.div(self.c, self.fold)

    def row_at(self, dy, dz):
        y = lax.rem(self.y + dy, self.lay["y_lo"])
        z = lax.rem(self.z + dz, self.nz)
        return y * self.nz + z

    def at_z(self, dz):
        return (self.row_at(0, dz), self.c)

    def at_far(self, d, dy):
        return (self.row_at(dy, NEAR * d), self.c)

    def at_col(self, k):
        return (self.r, lax.rem(self.c + k, self.ncol))

    def at_fold(self, k):
        inner = lax.rem(self.c, self.fold)
        return (self.r, self.y_hi * self.fold + lax.rem(inner + k, self.fold))

    def at_y(self, k):
        y_lo = self.lay["y_lo"]
        y = lax.rem(self.y_hi * y_lo + self.y + k, self.ny)
        inner = lax.rem(self.c, self.fold)
        return (
            lax.rem(y, y_lo) * self.nz + self.z,
            lax.div(y, y_lo) * self.fold + inner,
        )

    def near_out(self):
        odd = lax.rem(self.z, 2)
        return (1, self.nz - 1, 2 + odd * (self.nz - 4))

    def near_in(self):
        odd = lax.rem(self.z, 2)
        return (self.nz - 1, 1, self.nz - 2 + odd * 4)


def split(values):
    high = values.astype(BF16)
    low = (values - high.astype(F32)).astype(BF16)
    return high, low


def apply_tile(vectors, weights):
    high, low = split(vectors)
    both = jnp.dot(jnp.concatenate([high, low], axis=0), weights, preferred_element_type=F32)
    width = weights.shape[1] // 2
    rows = vectors.shape[0]
    high_part = both[:rows, :width] + both[:rows, width:]
    return high_part + (both[rows:, :width] + both[rows:, width:])


def dot_nt(a, b):
    return lax.dot_general(
        a, b, (((1,), (1,)), ((), ())), precision=HIGH, preferred_element_type=F32
    )


def dot_nn(a, b):
    return jnp.dot(a, b, precision=HIGH, preferred_element_type=F32)


def normalise(gram, rows):
    count = gram.shape[0]
    tall = lax.broadcasted_iota(jnp.int32, (count, 1), 0)
    row_id = lax.broadcasted_iota(jnp.int32, rows.shape, 0)
    for j in range(count):
        inverse = 1.0 / jnp.sqrt(gram[j : j + 1, j : j + 1])
        column = jnp.where(tall > j, gram[:, j : j + 1] * inverse, 0.0)
        across = gram[j : j + 1, :] * inverse
        pivot = rows[j : j + 1, :] * inverse
        rows = jnp.where(row_id == j, jnp.broadcast_to(pivot, rows.shape), rows - column * pivot)
        gram = gram - column * across
    return rows


def kernel(
    lay,
    total_len,
    cur_ref,
    prior_ref,
    diag_ref,
    tiles_hbm,
    where_ref,
    count_ref,
    out_ref,
    tiles,
    w_cols,
    w_rows,
    vec,
    far_in,
    col_in,
    terms,
    near_got,
    partial,
    far_got,
    col_terms,
    col_got,
    sums,
    fold_got,
    y_got,
    z_got,
    gb_sums,
    gb_fold,
    gb_y,
    gb_z,
    basis,
    cross,
    gmat,
    tile_sem,
    recv,
    gb_recv,
    sent,
    gb_sent,
):
    p = Place(lay)
    y_lo, z_far = lay["y_lo"], lay["z_far"]
    far = y_lo * z_far
    slots = tiles.shape[0]
    width = tiles.shape[1]
    k_rows = cur_ref.shape[0]

    barrier = pltpu.get_barrier_semaphore()
    greet = [p.at_z(dz) for dz in range(1, p.nz)]
    greet += [p.at_far(d, dy) for d in range(z_far) for dy in range(1, y_lo)]
    greet += [p.at_col(k) for k in range(1, p.ncol)]
    for k in range(1, p.ny):
        if k != y_lo and lay["y_hi"] > 1:
            greet.append(p.at_y(k))
    for device in greet:
        pl.semaphore_signal(barrier, inc=1, device_id=device, device_id_type=MESH)

    fetch = pltpu.make_async_copy(tiles_hbm, tiles, tile_sem)
    fetch.start()

    n_basis = prior_ref.shape[0] + k_rows
    basis[...] = jnp.zeros(basis.shape, F32)
    cross[...] = jnp.zeros(cross.shape, F32)
    gmat[...] = jnp.zeros(gmat.shape, F32)
    basis[0, k_rows : n_basis] = prior_ref[...]
    basis[0, n_basis : n_basis + k_rows] = cur_ref[...]
    own = dot_nt(basis[0, k_rows : n_basis + k_rows], basis[0])
    packed = own[0:16] + pltpu.roll(own[16:32], 40, 1)
    packed = packed + jnp.concatenate(
        [pltpu.roll(own[32:40], 80, 1), jnp.zeros((8, width), F32)], axis=0
    )
    gb_sums[0] = packed
    vec[0] = cur_ref[...]
    far_in[0, 0, 0] = cur_ref[...]
    col_in[0, 0] = cur_ref[...]

    pl.semaphore_wait(barrier, len(greet))

    def send(src, dst, send_sem, recv_sem, device):
        pltpu.make_async_remote_copy(
            src_ref=src,
            dst_ref=dst,
            send_sem=send_sem,
            recv_sem=recv_sem,
            device_id=device,
            device_id_type=MESH,
        ).start()

    def wait_for(ref, sem):
        pltpu.make_async_copy(ref, ref, sem).wait()

    far_order = [d for d in (2, 1, 3) if d < z_far] + [0]
    near_order = [d for d in (0, 1, 3, 2) if d < z_far]

    def gather_start(s):
        for d in far_order:
            for dy in range(y_lo):
                if d or dy:
                    send(
                        vec.at[s],
                        far_in.at[s, 0, d * y_lo + dy],
                        sent.at[s, 0],
                        recv.at[s, d],
                        p.at_far(d, dy),
                    )
        for k in range(1, p.ncol):
            send(vec.at[s], col_in.at[s, k], sent.at[s, 1], recv.at[s, 4], p.at_col(k))

    def gather_rest(s):
        for d in near_order:
            first = 1 if d == 0 else 0
            arrived = far_in.at[s, 0, pl.ds(d * y_lo + first, y_lo - first)]
            wait_for(arrived, recv.at[s, d])
            chunk = pl.ds(d * y_lo, y_lo)
            for q, dz in enumerate(p.near_out()):
                send(
                    far_in.at[s, 0, chunk],
                    far_in.at[s, 1 + q, chunk],
                    sent.at[s, 2],
                    recv.at[s, 5],
                    p.at_z(dz),
                )
        wait_for(col_in.at[s, pl.ds(1, p.ncol - 1)], recv.at[s, 4])
        wait_for(far_in.at[s, pl.ds(1, 3)], recv.at[s, 5])

    def all_sum_stage(s, stage, value, got, ids, sem_s, sem_r, source):
        source[stage] = value
        for k, device in enumerate(ids):
            send(source.at[stage], got.at[k], sem_s, sem_r, device)

    def all_sum_wait(value, got, count, sem_r):
        wait_for(got, sem_r)
        total = value
        for k in range(count):
            total = total + got[k]
        return total

    fold_ids = [p.at_fold(k) for k in range(1, p.fold)]
    y_ids = [p.at_y(k) for k in range(1, p.ny)]
    z_ids = [p.at_z(k) for k in range(1, p.nz)]

    gather_start(0)
    for k, device in enumerate(fold_ids):
        send(gb_sums.at[0], gb_fold.at[k], gb_sent.at[0], gb_recv.at[0], device)

    fetch.wait()
    count = count_ref[0, 0]

    def prepare(t, carry):
        tile = tiles[t]
        tile = jnp.where(t < count, tile, jnp.zeros_like(tile))
        high, low = split(tile)
        w_cols[t] = jnp.concatenate([high, low], axis=1)
        high, low = split(tile.T)
        w_rows[t] = jnp.concatenate([high, low], axis=1)
        return carry

    lax.fori_loop(0, slots, prepare, 0)

    near_out, near_in = p.near_out(), p.near_in()
    row_slot, far_slot, row_goal, far_goal = [], [], [], []
    for t in range(slots):
        at_row, at_col = where_ref[0, t], where_ref[1, t]
        row_slot.append(lax.rem(p.c - at_row + p.ncol, p.ncol))
        row_goal.append(lax.rem(at_row - p.c + p.ncol, p.ncol))
        y_t = lax.div(at_col, p.nz)
        z_t = lax.rem(at_col, p.nz)
        far_t = lax.div(z_t, NEAR)
        near_t = lax.rem(z_t, NEAR)
        slot = jnp.int32(0)
        goals = []
        dy_in = lax.rem(p.y - y_t + y_lo, y_lo)
        dy_out = lax.rem(y_t - p.y + y_lo, y_lo)
        for q in range(4):
            z_from = p.z if q == 0 else lax.rem(p.z + near_in[q - 1], p.nz)
            z_to = p.z if q == 0 else lax.rem(p.z + near_out[q - 1], p.nz)
            d_in = lax.rem(lax.div(z_from, NEAR) - far_t + z_far, z_far)
            here = q * far + d_in * y_lo + dy_in
            slot = jnp.where(lax.rem(z_from, NEAR) == near_t, here, slot)
            d_out = lax.rem(far_t - lax.div(z_to, NEAR) + z_far, z_far)
            there = d_out * y_lo + dy_out
            goals.append(jnp.where(lax.rem(z_to, NEAR) == near_t, there, -1))
        far_slot.append(slot)
        far_goal.append(goals)
    block_id = lax.broadcasted_iota(jnp.int32, (y_lo, k_rows, width), 0)
    col_id = lax.broadcasted_iota(jnp.int32, (p.ncol, k_rows, width), 0)

    def multiply(s):
        flat = far_in.at[s]
        to_cols = [apply_tile(col_in[s, row_slot[t]], w_cols[t]) for t in range(slots)]
        for d in far_order:
            for q in (1, 2, 3, 0):
                block = jnp.zeros(block_id.shape, F32)
                for t in range(slots):
                    hit = block_id == far_goal[t][q] - d * y_lo
                    block = block + jnp.where(hit, to_cols[t][None], 0.0)
                chunk = pl.ds(d * y_lo, y_lo)
                terms[s, q, chunk] = block
                if q:
                    send(
                        terms.at[s, q, chunk],
                        near_got.at[s, q - 1, chunk],
                        sent.at[s, 3],
                        recv.at[s, 6 + d],
                        p.at_z(near_out[q - 1]),
                    )
        block = jnp.zeros(col_id.shape, F32)
        for t in range(slots):
            q_t = lax.div(far_slot[t], far)
            to_rows = apply_tile(flat[q_t, lax.rem(far_slot[t], far)], w_rows[t])
            block = block + jnp.where(col_id == row_goal[t], to_rows[None], 0.0)
        col_terms[s] = block
        for k in range(1, p.ncol):
            send(col_terms.at[s, k], col_got.at[s, k - 1], sent.at[s, 4], recv.at[s, 10], p.at_col(k))

    def collect(s):
        for d in far_order:
            chunk = pl.ds(d * y_lo, y_lo)
            wait_for(near_got.at[s, pl.ds(0, 3), chunk], recv.at[s, 6 + d])
            total = terms[s, 0, chunk]
            for q in range(3):
                total = total + near_got[s, q, chunk]
            partial[s, chunk] = total
            for dy in range(y_lo):
                if d or dy:
                    at = d * y_lo + dy
                    send(partial.at[s, at], far_got.at[s, at - 1], sent.at[s, 5], recv.at[s, 11], p.at_far(d, dy))
        image = diag_ref[...] * vec[s] + col_terms[s, 0] + partial[s, 0]
        wait_for(col_got.at[s], recv.at[s, 10])
        for k in range(p.ncol - 1):
            image = image + col_got[s, k]
        wait_for(far_got.at[s], recv.at[s, 11])
        for k in range(far - 1):
            image = image + far_got[s, k]
        return image

    def gb_stage(value, stage, ids, got):
        gb_sums[stage] = value
        for k, device in enumerate(ids):
            send(gb_sums.at[stage], got.at[k], gb_sent.at[stage], gb_recv.at[stage], device)

    def gb_total(stage, got, n):
        wait_for(got, gb_recv.at[stage])
        total = gb_sums[stage]
        for k in range(n):
            total = total + got[k]
        return total

    lane = lax.broadcasted_iota(jnp.int32, (k_rows, width), 1)
    in_basis = (lane >= k_rows) & (lane < k_rows + n_basis)

    for s in range(2):
        if s:
            gather_start(s)
        gather_rest(s)
        multiply(s)
        if s == 0:
            gb_stage(gb_total(0, gb_fold, p.fold - 1), 1, y_ids, gb_y)
        image = collect(s)
        basis[s, 0:k_rows] = image
        value = dot_nt(image, basis[s])
        if s:
            value = value + dot_nt(vec[s], cross[...])
        all_sum_stage(s, 0, value, fold_got.at[s], fold_ids, sent.at[s, 6], recv.at[s, 12], sums.at[s])
        if s == 0:
            gb_stage(gb_total(1, gb_y, p.ny - 1), 2, z_ids, gb_z)
        value = all_sum_wait(value, fold_got.at[s], p.fold - 1, recv.at[s, 12])
        all_sum_stage(s, 1, value, y_got.at[s], y_ids, sent.at[s, 7], recv.at[s, 13], sums.at[s])
        value = all_sum_wait(value, y_got.at[s], p.ny - 1, recv.at[s, 13])
        all_sum_stage(s, 2, value, z_got.at[s], z_ids, sent.at[s, 8], recv.at[s, 14], sums.at[s])
        if s == 0:
            packed = gb_total(2, gb_z, p.nz - 1)
            wide = lax.broadcasted_iota(jnp.int32, packed.shape, 1)
            keep = (wide >= 8) & (wide < 48)
            gmat[0, 8:24] = jnp.where(keep, packed, 0.0)
            gmat[0, 24:40] = jnp.where(keep, pltpu.roll(packed, width - 40, 1), 0.0)
            gmat[0, 40:48] = jnp.where(keep, pltpu.roll(packed, width - 80, 1), 0.0)[0:8]
        value = all_sum_wait(value, z_got.at[s], p.nz - 1, recv.at[s, 14])

        inner = jnp.where(in_basis, value, 0.0)
        proj = inner * (1.0 / total_len)
        if s:
            newest = jnp.where(in_basis, pltpu.roll(value, width - 64, 1), 0.0)
            gmat[1, 40:48] = jnp.where(lane < 40, newest, 0.0)
            gmat[2, 40:48] = newest
            swept = dot_nn(proj, gmat[1]) + dot_nt(proj, gmat[2])
        else:
            swept = dot_nn(proj, gmat[0])
        gram = (value[:, 0:k_rows] + dot_nt(swept - 2.0 * inner, proj)) * (1.0 / total_len)
        remainder = image - dot_nn(proj, basis[s])
        fresh = normalise(gram, remainder)
        out_ref[s * k_rows : (s + 1) * k_rows] = fresh
        if s == 0:
            vec[1] = fresh
            far_in[1, 0, 0] = fresh
            col_in[1, 0] = fresh
            basis[1, 8:32] = prior_ref[8:32]
            basis[1, 32:40] = cur_ref[...]
            basis[1, 40:48] = fresh
            cross[72:112] = basis[1, 8:48]
            old = pltpu.roll(gmat[0, 16:48], width - 8, 1)
            wide = lax.broadcasted_iota(jnp.int32, old.shape, 1)
            gmat[1, 8:40] = jnp.where((wide >= 8) & (wide < 40), old, 0.0)

    for s in range(2):
        wait_for(far_in.at[s, 0, pl.ds(0, far - 1)], sent.at[s, 0])
        wait_for(col_in.at[s, pl.ds(1, p.ncol - 1)], sent.at[s, 1])
        wait_for(far_in.at[s, pl.ds(1, 3)], sent.at[s, 2])
        wait_for(near_got.at[s], sent.at[s, 3])
        wait_for(col_got.at[s], sent.at[s, 4])
        wait_for(far_got.at[s], sent.at[s, 5])
        wait_for(fold_got.at[s], sent.at[s, 6])
        wait_for(y_got.at[s], sent.at[s, 7])
        wait_for(z_got.at[s], sent.at[s, 8])
    wait_for(gb_fold, gb_sent.at[0])
    wait_for(gb_y, gb_sent.at[1])
    wait_for(gb_z, gb_sent.at[2])


def body(lay, total_len, current_block, prior_blocks, diagonal, stored_tiles, tile_coords, tile_counts):
    k_rows, width = current_block.shape
    slots = stored_tiles.shape[2]
    far = lay["y_lo"] * lay["z_far"]
    fold = lay["x"] * lay["core"]
    ncol = lay["y_hi"] * fold
    ny = lay["y_lo"] * lay["y_hi"]
    nz = lay["z_far"] * NEAR
    one = (k_rows, width)
    vmem = pl.BlockSpec(memory_space=pltpu.VMEM)
    smem = pl.BlockSpec(memory_space=pltpu.SMEM)
    scratch = [
        pltpu.VMEM((slots, width, width), F32),
        pltpu.VMEM((slots, width, 2 * width), BF16),
        pltpu.VMEM((slots, width, 2 * width), BF16),
        pltpu.VMEM((2, *one), F32),
        pltpu.VMEM((2, 4, far, *one), F32),
        pltpu.VMEM((2, ncol, *one), F32),
        pltpu.VMEM((2, 4, far, *one), F32),
        pltpu.VMEM((2, 3, far, *one), F32),
        pltpu.VMEM((2, far, *one), F32),
        pltpu.VMEM((2, far - 1, *one), F32),
        pltpu.VMEM((2, ncol, *one), F32),
        pltpu.VMEM((2, ncol - 1, *one), F32),
        pltpu.VMEM((2, 3, *one), F32),
        pltpu.VMEM((2, fold - 1, *one), F32),
        pltpu.VMEM((2, ny - 1, *one), F32),
        pltpu.VMEM((2, nz - 1, *one), F32),
        pltpu.VMEM((3, 2 * k_rows, width), F32),
        pltpu.VMEM((fold - 1, 2 * k_rows, width), F32),
        pltpu.VMEM((ny - 1, 2 * k_rows, width), F32),
        pltpu.VMEM((nz - 1, 2 * k_rows, width), F32),
        pltpu.VMEM((2, width, width), F32),
        pltpu.VMEM((width, width), F32),
        pltpu.VMEM((3, width, width), F32),
        pltpu.SemaphoreType.DMA,
        pltpu.SemaphoreType.DMA((2, 15)),
        pltpu.SemaphoreType.DMA((3,)),
        pltpu.SemaphoreType.DMA((2, 9)),
        pltpu.SemaphoreType.DMA((3,)),
    ]
    return pl.pallas_call(
        functools.partial(kernel, lay, total_len),
        out_shape=jax.ShapeDtypeStruct((2 * k_rows, width), F32),
        in_specs=[vmem, vmem, vmem, pl.BlockSpec(memory_space=pl.ANY), smem, smem],
        out_specs=vmem,
        scratch_shapes=scratch,
        compiler_params=pltpu.CompilerParams(
            collective_id=0, has_side_effects=True, vmem_limit_bytes=24 * 1024 * 1024
        ),
        name="lanczos",
    )(
        current_block,
        prior_blocks,
        diagonal[None, :],
        stored_tiles[0, 0],
        tile_coords[0, 0],
        tile_counts,
    )


def build(mesh, lay):
    total_len = float(128 * mesh.shape["row"] * mesh.shape["col"])
    in_specs = (
        P(None, ("row", "col")),
        P(None, ("row", "col")),
        P(("row", "col")),
        P("row", "col", None, None, None),
        P("row", "col", None, None),
        P("row", "col"),
    )
    return jax.shard_map(
        functools.partial(body, lay, total_len),
        mesh=mesh,
        in_specs=in_specs,
        out_specs=P(None, ("row", "col")),
        check_vma=False,
    )


def solution(mesh):
    return build(mesh, LAYOUT)
```

```python
import functools

import jax
import jax.numpy as jnp
from jax import lax
from jax.experimental import pallas as pl
from jax.experimental.pallas import tpu as pltpu
from jax.sharding import PartitionSpec as P

MESH = pl.DeviceIdType.MESH
HIGH = lax.Precision.HIGHEST
F32 = jnp.float32
BF16 = jnp.bfloat16

LAYOUT = dict(y_lo=4, z_far=4, y_hi=2, x=4, core=2)
NEAR = 4


class Place:
    def __init__(self, lay):
        self.lay = lay
        self.nz = lay["z_far"] * NEAR
        self.ncol = lay["y_hi"] * lay["x"] * lay["core"]
        self.fold = lay["x"] * lay["core"]
        self.ny = lay["y_lo"] * lay["y_hi"]
        self.r = lax.axis_index("row")
        self.c = lax.axis_index("col")
        self.y = lax.div(self.r, self.nz)
        self.z = lax.rem(self.r, self.nz)
        self.z_far = lax.div(self.z, NEAR)
        self.z_near = lax.rem(self.z, NEAR)
        self.y_hi = lax.div(self.c, self.fold)

    def row_at(self, dy, dz):
        y = lax.rem(self.y + dy, self.lay["y_lo"])
        z = lax.rem(self.z + dz, self.nz)
        return y * self.nz + z

    def at_z(self, dz):
        return (self.row_at(0, dz), self.c)

    def at_far(self, d, dy):
        return (self.row_at(dy, NEAR * d), self.c)

    def at_col(self, k):
        return (self.r, lax.rem(self.c + k, self.ncol))

    def at_fold(self, k):
        inner = lax.rem(self.c, self.fold)
        return (self.r, self.y_hi * self.fold + lax.rem(inner + k, self.fold))

    def at_y(self, k):
        y_lo = self.lay["y_lo"]
        y = lax.rem(self.y_hi * y_lo + self.y + k, self.ny)
        inner = lax.rem(self.c, self.fold)
        return (
            lax.rem(y, y_lo) * self.nz + self.z,
            lax.div(y, y_lo) * self.fold + inner,
        )

    def near_out(self):
        odd = lax.rem(self.z, 2)
        return (1, self.nz - 1, 2 + odd * (self.nz - 4))

    def near_in(self):
        odd = lax.rem(self.z, 2)
        return (self.nz - 1, 1, self.nz - 2 + odd * 4)


def split(values):
    high = values.astype(BF16)
    low = (values - high.astype(F32)).astype(BF16)
    return high, low


def apply_tile(vectors, weights):
    high, low = split(vectors)
    both = jnp.dot(jnp.concatenate([high, low], axis=0), weights, preferred_element_type=F32)
    width = weights.shape[1] // 2
    rows = vectors.shape[0]
    high_part = both[:rows, :width] + both[:rows, width:]
    return high_part + (both[rows:, :width] + both[rows:, width:])


def dot_nt(a, b):
    return lax.dot_general(
        a, b, (((1,), (1,)), ((), ())), precision=HIGH, preferred_element_type=F32
    )


def dot_nn(a, b):
    return jnp.dot(a, b, precision=HIGH, preferred_element_type=F32)


def normalise(gram, rows):
    count = gram.shape[0]
    tall = lax.broadcasted_iota(jnp.int32, (count, 1), 0)
    row_id = lax.broadcasted_iota(jnp.int32, rows.shape, 0)
    for j in range(count):
        inverse = 1.0 / jnp.sqrt(gram[j : j + 1, j : j + 1])
        column = jnp.where(tall > j, gram[:, j : j + 1] * inverse, 0.0)
        across = gram[j : j + 1, :] * inverse
        pivot = rows[j : j + 1, :] * inverse
        rows = jnp.where(row_id == j, jnp.broadcast_to(pivot, rows.shape), rows - column * pivot)
        gram = gram - column * across
    return rows


def kernel(
    lay,
    total_len,
    cur_ref,
    prior_ref,
    diag_ref,
    tiles_hbm,
    where_ref,
    count_ref,
    out_ref,
    tiles,
    w_cols,
    w_rows,
    vec,
    far_first,
    far_second,
    col_first,
    col_second,
    terms,
    near_got,
    partial,
    far_got,
    col_terms,
    col_got,
    sums,
    fold_got,
    y_got,
    z_got,
    gb_sums,
    gb_fold,
    gb_y,
    gb_z,
    basis,
    cross,
    gmat,
    image_ref,
    far_b,
    col_b,
    y_cols,
    y_rows,
    tile_sem,
    recv,
    gb_recv,
    sent,
    gb_sent,
    b_recv,
    b_sent,
):
    p = Place(lay)
    far_in, col_in = (far_first, far_second), (col_first, col_second)
    y_lo, z_far = lay["y_lo"], lay["z_far"]
    far = y_lo * z_far
    slots = tiles.shape[0]
    width = tiles.shape[1]
    k_rows = cur_ref.shape[0]

    barrier = pltpu.get_barrier_semaphore()
    greet = [p.at_z(dz) for dz in range(1, p.nz)]
    greet += [p.at_far(d, dy) for d in range(z_far) for dy in range(1, y_lo)]
    greet += [p.at_col(k) for k in range(1, p.ncol)]
    for k in range(1, p.ny):
        if k != y_lo and lay["y_hi"] > 1:
            greet.append(p.at_y(k))
    for device in greet:
        pl.semaphore_signal(barrier, inc=1, device_id=device, device_id_type=MESH)

    fetch = pltpu.make_async_copy(tiles_hbm, tiles, tile_sem)
    fetch.start()

    n_basis = prior_ref.shape[0] + k_rows
    basis[...] = jnp.zeros(basis.shape, F32)
    cross[...] = jnp.zeros(cross.shape, F32)
    gmat[...] = jnp.zeros(gmat.shape, F32)
    basis[0, k_rows : n_basis] = prior_ref[...]
    basis[0, n_basis : n_basis + k_rows] = cur_ref[...]
    own = dot_nt(basis[0, k_rows : n_basis + k_rows], basis[0])
    packed = own[0:16] + pltpu.roll(own[16:32], 40, 1)
    packed = packed + jnp.concatenate(
        [pltpu.roll(own[32:40], 80, 1), jnp.zeros((8, width), F32)], axis=0
    )
    gb_sums[0] = packed
    vec[0] = cur_ref[...]
    far_in[0][0, 0] = cur_ref[...]
    col_in[0][0] = cur_ref[...]

    pl.semaphore_wait(barrier, len(greet))

    def send(src, dst, send_sem, recv_sem, device):
        pltpu.make_async_remote_copy(
            src_ref=src,
            dst_ref=dst,
            send_sem=send_sem,
            recv_sem=recv_sem,
            device_id=device,
            device_id_type=MESH,
        ).start()

    def wait_for(ref, sem):
        pltpu.make_async_copy(ref, ref, sem).wait()

    far_order = [d for d in (2, 1, 3) if d < z_far] + [0]
    near_order = [d for d in (0, 1, 3, 2) if d < z_far]

    def gather_start(s):
        source = image_ref if s else vec.at[0]
        for d in far_order:
            for dy in range(y_lo):
                if d or dy:
                    send(
                        source,
                        far_in[s].at[0, d * y_lo + dy],
                        sent.at[s, 0],
                        recv.at[s, d],
                        p.at_far(d, dy),
                    )
        for k in range(1, p.ncol):
            send(source, col_in[s].at[k], sent.at[s, 1], recv.at[s, 4], p.at_col(k))

    def gather_chunks(s, order):
        for d in order:
            first = 1 if d == 0 else 0
            arrived = far_in[s].at[0, pl.ds(d * y_lo + first, y_lo - first)]
            wait_for(arrived, recv.at[s, d])
            chunk = pl.ds(d * y_lo, y_lo)
            for q, dz in enumerate(p.near_out()):
                send(
                    far_in[s].at[0, chunk],
                    far_in[s].at[1 + q, chunk],
                    sent.at[s, 2],
                    recv.at[s, 5],
                    p.at_z(dz),
                )

    def gather_end(s):
        wait_for(col_in[s].at[pl.ds(1, p.ncol - 1)], recv.at[s, 4])
        wait_for(far_in[s].at[pl.ds(1, 3)], recv.at[s, 5])

    direct = [d for d in range(z_far) if d != 2]
    half = y_lo // 2

    def prior_start():
        if lay["y_hi"] > 1:
            send(prior_ref, col_b.at[0, 1], b_sent.at[0], b_recv.at[0], p.at_col(p.fold))
        for d in direct:
            for dy in range(y_lo):
                if d or dy:
                    send(prior_ref, far_b.at[0, d * y_lo + dy], b_sent.at[1], b_recv.at[1 + d], p.at_far(d, dy))

    def prior_near(d):
        chunk = pl.ds(d * y_lo, y_lo)
        for q, dz in enumerate(p.near_out()):
            send(far_b.at[0, chunk], far_b.at[1 + q, chunk], b_sent.at[2], b_recv.at[5], p.at_z(dz))

    def prior_middle():
        if lay["y_hi"] > 1:
            wait_for(col_b.at[0, 1], b_recv.at[0])
        for k in range(1, p.fold):
            send(col_b.at[0], col_b.at[k], b_sent.at[3], b_recv.at[6], p.at_fold(k))
        for d in direct:
            first = 1 if d == 0 else 0
            wait_for(far_b.at[0, pl.ds(d * y_lo + first, y_lo - first)], b_recv.at[1 + d])
        if z_far > 2:
            for d, first in ((1, 0), (3, half)):
                send(
                    far_b.at[0, pl.ds(d * y_lo + first, half)],
                    far_b.at[0, pl.ds(2 * y_lo + first, half)],
                    b_sent.at[4],
                    b_recv.at[3],
                    p.at_far(d, 0),
                )
        for d in direct:
            prior_near(d)

    def prior_late():
        if z_far > 2:
            wait_for(far_b.at[0, pl.ds(2 * y_lo, y_lo)], b_recv.at[3])
            prior_near(2)

    def prior_end():
        wait_for(col_b.at[pl.ds(1, p.fold - 1)], b_recv.at[6])
        wait_for(far_b.at[pl.ds(1, 3)], b_recv.at[5])

    def all_sum_stage(s, stage, value, got, ids, sem_s, sem_r, source):
        source[stage] = value
        for k, device in enumerate(ids):
            send(source.at[stage], got.at[k], sem_s, sem_r, device)

    def all_sum_wait(value, got, count, sem_r):
        wait_for(got, sem_r)
        total = value
        for k in range(count):
            total = total + got[k]
        return total

    fold_ids = [p.at_fold(k) for k in range(1, p.fold)]
    y_ids = [p.at_y(k) for k in range(1, p.ny)]
    z_ids = [p.at_z(k) for k in range(1, p.nz)]

    gather_start(0)
    far_b[0, 0] = prior_ref[...]
    col_b[0, 0] = prior_ref[...]
    prior_start()
    for k, device in enumerate(fold_ids):
        send(gb_sums.at[0], gb_fold.at[k], gb_sent.at[0], gb_recv.at[0], device)

    fetch.wait()
    count = count_ref[0, 0]

    def prepare(t, carry):
        tile = tiles[t]
        tile = jnp.where(t < count, tile, jnp.zeros_like(tile))
        high, low = split(tile)
        w_cols[t] = jnp.concatenate([high, low], axis=1)
        high, low = split(tile.T)
        w_rows[t] = jnp.concatenate([high, low], axis=1)
        return carry

    lax.fori_loop(0, slots, prepare, 0)

    near_out, near_in = p.near_out(), p.near_in()
    row_slot, far_slot, row_goal, far_goal, row_part = [], [], [], [], []
    for t in range(slots):
        at_row, at_col = where_ref[0, t], where_ref[1, t]
        row_slot.append(lax.rem(p.c - at_row + p.ncol, p.ncol))
        turn = lax.rem(p.c - at_row + p.ncol, p.fold)
        away = jnp.where(lax.div(at_row, p.fold) == p.y_hi, 0, 1)
        row_part.append((turn, away))
        row_goal.append(lax.rem(at_row - p.c + p.ncol, p.ncol))
        y_t = lax.div(at_col, p.nz)
        z_t = lax.rem(at_col, p.nz)
        far_t = lax.div(z_t, NEAR)
        near_t = lax.rem(z_t, NEAR)
        slot = jnp.int32(0)
        goals = []
        dy_in = lax.rem(p.y - y_t + y_lo, y_lo)
        dy_out = lax.rem(y_t - p.y + y_lo, y_lo)
        for q in range(4):
            z_from = p.z if q == 0 else lax.rem(p.z + near_in[q - 1], p.nz)
            z_to = p.z if q == 0 else lax.rem(p.z + near_out[q - 1], p.nz)
            d_in = lax.rem(lax.div(z_from, NEAR) - far_t + z_far, z_far)
            here = q * far + d_in * y_lo + dy_in
            slot = jnp.where(lax.rem(z_from, NEAR) == near_t, here, slot)
            d_out = lax.rem(far_t - lax.div(z_to, NEAR) + z_far, z_far)
            there = d_out * y_lo + dy_out
            goals.append(jnp.where(lax.rem(z_to, NEAR) == near_t, there, -1))
        far_slot.append(slot)
        far_goal.append(goals)
    block_id = lax.broadcasted_iota(jnp.int32, (y_lo, k_rows, width), 0)
    col_id = lax.broadcasted_iota(jnp.int32, (p.ncol, k_rows, width), 0)

    def far_at(t):
        return lax.div(far_slot[t], far), lax.rem(far_slot[t], far)

    def widen(t):
        turn, away = row_part[t]
        q, at = far_at(t)
        for got, old, weights, kept in (
            (col_in[1][row_slot[t]], col_b[turn, away], w_cols, y_cols),
            (far_in[1][q, at], far_b[q, at], w_rows, y_rows),
        ):
            kept[t, 0:40] = apply_tile(jnp.concatenate([got, old], axis=0), weights[t])

    def multiply(s, mix):
        if s:
            to_cols = [dot_nn(mix, y_cols[t]) for t in range(slots)]
        else:
            to_cols = [apply_tile(col_in[0][row_slot[t]], w_cols[t]) for t in range(slots)]
        for d in far_order:
            for q in (1, 2, 3, 0):
                block = jnp.zeros(block_id.shape, F32)
                for t in range(slots):
                    hit = block_id == far_goal[t][q] - d * y_lo
                    block = block + jnp.where(hit, to_cols[t][None], 0.0)
                chunk = pl.ds(d * y_lo, y_lo)
                terms[s, q, chunk] = block
                if q:
                    send(
                        terms.at[s, q, chunk],
                        near_got.at[s, q - 1, chunk],
                        sent.at[s, 3],
                        recv.at[s, 6 + d],
                        p.at_z(near_out[q - 1]),
                    )
        block = jnp.zeros(col_id.shape, F32)
        for t in range(slots):
            if s:
                to_rows = dot_nn(mix, y_rows[t])
            else:
                q, at = far_at(t)
                to_rows = apply_tile(far_in[0][q, at], w_rows[t])
                y_rows[t, 40:48] = to_rows
                y_cols[t, 40:48] = to_cols[t]
            block = block + jnp.where(col_id == row_goal[t], to_rows[None], 0.0)
        col_terms[s] = block
        for k in range(1, p.ncol):
            send(col_terms.at[s, k], col_got.at[s, k - 1], sent.at[s, 4], recv.at[s, 10], p.at_col(k))

    def collect(s):
        for d in far_order:
            chunk = pl.ds(d * y_lo, y_lo)
            wait_for(near_got.at[s, pl.ds(0, 3), chunk], recv.at[s, 6 + d])
            total = terms[s, 0, chunk]
            for q in range(3):
                total = total + near_got[s, q, chunk]
            partial[s, chunk] = total
            for dy in range(y_lo):
                if d or dy:
                    at = d * y_lo + dy
                    send(partial.at[s, at], far_got.at[s, at - 1], sent.at[s, 5], recv.at[s, 11], p.at_far(d, dy))
        image = diag_ref[...] * vec[s] + col_terms[s, 0] + partial[s, 0]
        wait_for(col_got.at[s], recv.at[s, 10])
        for k in range(p.ncol - 1):
            image = image + col_got[s, k]
        wait_for(far_got.at[s], recv.at[s, 11])
        for k in range(far - 1):
            image = image + far_got[s, k]
        return image

    def gb_stage(value, stage, ids, got):
        gb_sums[stage] = value
        for k, device in enumerate(ids):
            send(gb_sums.at[stage], got.at[k], gb_sent.at[stage], gb_recv.at[stage], device)

    def gb_total(stage, got, n):
        wait_for(got, gb_recv.at[stage])
        total = gb_sums[stage]
        for k in range(n):
            total = total + got[k]
        return total

    lane = lax.broadcasted_iota(jnp.int32, (k_rows, width), 1)
    in_basis = (lane >= k_rows) & (lane < k_rows + n_basis)

    gather_chunks(0, near_order)
    gather_end(0)
    mix = None
    for s in range(2):
        multiply(s, mix)
        if s == 0:
            gb_stage(gb_total(0, gb_fold, p.fold - 1), 1, y_ids, gb_y)
            prior_middle()
        image = collect(s)
        basis[s, 0:k_rows] = image
        value = dot_nt(image, basis[s])
        if s:
            value = value + dot_nt(vec[s], cross[...])
        all_sum_stage(s, 0, value, fold_got.at[s], fold_ids, sent.at[s, 6], recv.at[s, 12], sums.at[s])
        if s == 0:
            image_ref[...] = image
            far_in[1][0, 0] = image
            col_in[1][0] = image
            gather_start(1)
            gb_stage(gb_total(1, gb_y, p.ny - 1), 2, z_ids, gb_z)
            prior_late()
        value = all_sum_wait(value, fold_got.at[s], p.fold - 1, recv.at[s, 12])
        all_sum_stage(s, 1, value, y_got.at[s], y_ids, sent.at[s, 7], recv.at[s, 13], sums.at[s])
        if s == 0:
            gather_chunks(1, near_order[:1])
        value = all_sum_wait(value, y_got.at[s], p.ny - 1, recv.at[s, 13])
        all_sum_stage(s, 2, value, z_got.at[s], z_ids, sent.at[s, 8], recv.at[s, 14], sums.at[s])
        if s == 0:
            gather_chunks(1, near_order[1:])
            packed = gb_total(2, gb_z, p.nz - 1)
            wide = lax.broadcasted_iota(jnp.int32, packed.shape, 1)
            keep = (wide >= 8) & (wide < 48)
            gmat[0, 8:24] = jnp.where(keep, packed, 0.0)
            gmat[0, 24:40] = jnp.where(keep, pltpu.roll(packed, width - 40, 1), 0.0)
            gmat[0, 40:48] = jnp.where(keep, pltpu.roll(packed, width - 80, 1), 0.0)[0:8]
            prior_end()
            gather_end(1)
            for t in range(slots):
                widen(t)
        value = all_sum_wait(value, z_got.at[s], p.nz - 1, recv.at[s, 14])

        inner = jnp.where(in_basis, value, 0.0)
        proj = inner * (1.0 / total_len)
        if s:
            newest = jnp.where(in_basis, pltpu.roll(value, width - 64, 1), 0.0)
            gmat[1, 40:48] = jnp.where(lane < 40, newest, 0.0)
            gmat[2, 40:48] = newest
            swept = dot_nn(proj, gmat[1]) + dot_nt(proj, gmat[2])
        else:
            swept = dot_nn(proj, gmat[0])
        gram = (value[:, 0:k_rows] + dot_nt(swept - 2.0 * inner, proj)) * (1.0 / total_len)
        rows = image - dot_nn(proj, basis[s])
        if s == 0:
            unit = jnp.where(lane == lax.broadcasted_iota(jnp.int32, lane.shape, 0), 1.0, 0.0)
            rows = jnp.concatenate([rows, unit - proj], axis=1)
        rows = normalise(gram, rows)
        fresh = rows[:, 0:width]
        out_ref[s * k_rows : (s + 1) * k_rows] = fresh
        if s == 0:
            mix = rows[:, width : width + 48]
            vec[1] = fresh
            basis[1, 8:32] = prior_ref[8:32]
            basis[1, 32:40] = cur_ref[...]
            basis[1, 40:48] = fresh
            cross[72:112] = basis[1, 8:48]
            old = pltpu.roll(gmat[0, 16:48], width - 8, 1)
            wide = lax.broadcasted_iota(jnp.int32, old.shape, 1)
            gmat[1, 8:40] = jnp.where((wide >= 8) & (wide < 40), old, 0.0)

    for s in range(2):
        wait_for(far_in[s].at[0, pl.ds(0, far - 1)], sent.at[s, 0])
        wait_for(col_in[s].at[pl.ds(1, p.ncol - 1)], sent.at[s, 1])
        wait_for(far_in[s].at[pl.ds(1, 3)], sent.at[s, 2])
        wait_for(near_got.at[s], sent.at[s, 3])
        wait_for(col_got.at[s], sent.at[s, 4])
        wait_for(far_got.at[s], sent.at[s, 5])
        wait_for(fold_got.at[s], sent.at[s, 6])
        wait_for(y_got.at[s], sent.at[s, 7])
        wait_for(z_got.at[s], sent.at[s, 8])
    wait_for(gb_fold, gb_sent.at[0])
    wait_for(gb_y, gb_sent.at[1])
    wait_for(gb_z, gb_sent.at[2])
    if lay["y_hi"] > 1:
        wait_for(col_b.at[0, 1], b_sent.at[0])
    wait_for(far_b.at[0, pl.ds(0, len(direct) * y_lo - 1)], b_sent.at[1])
    wait_for(far_b.at[pl.ds(1, 3)], b_sent.at[2])
    wait_for(col_b.at[pl.ds(1, p.fold - 1)], b_sent.at[3])
    if z_far > 2:
        wait_for(far_b.at[0, pl.ds(2 * y_lo, y_lo)], b_sent.at[4])


def body(lay, total_len, current_block, prior_blocks, diagonal, stored_tiles, tile_coords, tile_counts):
    k_rows, width = current_block.shape
    slots = stored_tiles.shape[2]
    far = lay["y_lo"] * lay["z_far"]
    fold = lay["x"] * lay["core"]
    ncol = lay["y_hi"] * fold
    ny = lay["y_lo"] * lay["y_hi"]
    nz = lay["z_far"] * NEAR
    one = (k_rows, width)
    vmem = pl.BlockSpec(memory_space=pltpu.VMEM)
    smem = pl.BlockSpec(memory_space=pltpu.SMEM)
    scratch = [
        pltpu.VMEM((slots, width, width), F32),
        pltpu.VMEM((slots, width, 2 * width), BF16),
        pltpu.VMEM((slots, width, 2 * width), BF16),
        pltpu.VMEM((2, *one), F32),
        pltpu.VMEM((4, far, *one), F32),
        pltpu.VMEM((4, far, *one), F32),
        pltpu.VMEM((ncol, *one), F32),
        pltpu.VMEM((ncol, *one), F32),
        pltpu.VMEM((2, 4, far, *one), F32),
        pltpu.VMEM((2, 3, far, *one), F32),
        pltpu.VMEM((2, far, *one), F32),
        pltpu.VMEM((2, far - 1, *one), F32),
        pltpu.VMEM((2, ncol, *one), F32),
        pltpu.VMEM((2, ncol - 1, *one), F32),
        pltpu.VMEM((2, 3, *one), F32),
        pltpu.VMEM((2, fold - 1, *one), F32),
        pltpu.VMEM((2, ny - 1, *one), F32),
        pltpu.VMEM((2, nz - 1, *one), F32),
        pltpu.VMEM((3, 2 * k_rows, width), F32),
        pltpu.VMEM((fold - 1, 2 * k_rows, width), F32),
        pltpu.VMEM((ny - 1, 2 * k_rows, width), F32),
        pltpu.VMEM((nz - 1, 2 * k_rows, width), F32),
        pltpu.VMEM((2, width, width), F32),
        pltpu.VMEM((width, width), F32),
        pltpu.VMEM((3, width, width), F32),
        pltpu.VMEM(one, F32),
        pltpu.VMEM((4, far, 4 * k_rows, width), F32),
        pltpu.VMEM((fold, lay["y_hi"], 4 * k_rows, width), F32),
        pltpu.VMEM((slots, 48, width), F32),
        pltpu.VMEM((slots, 48, width), F32),
        pltpu.SemaphoreType.DMA,
        pltpu.SemaphoreType.DMA((2, 15)),
        pltpu.SemaphoreType.DMA((3,)),
        pltpu.SemaphoreType.DMA((2, 9)),
        pltpu.SemaphoreType.DMA((3,)),
        pltpu.SemaphoreType.DMA((7,)),
        pltpu.SemaphoreType.DMA((5,)),
    ]
    return pl.pallas_call(
        functools.partial(kernel, lay, total_len),
        out_shape=jax.ShapeDtypeStruct((2 * k_rows, width), F32),
        in_specs=[vmem, vmem, vmem, pl.BlockSpec(memory_space=pl.ANY), smem, smem],
        out_specs=vmem,
        scratch_shapes=scratch,
        compiler_params=pltpu.CompilerParams(
            collective_id=0, has_side_effects=True, vmem_limit_bytes=24 * 1024 * 1024
        ),
        name="lanczos",
    )(
        current_block,
        prior_blocks,
        diagonal[None, :],
        stored_tiles[0, 0],
        tile_coords[0, 0],
        tile_counts,
    )


def build(mesh, lay):
    total_len = float(128 * mesh.shape["row"] * mesh.shape["col"])
    in_specs = (
        P(None, ("row", "col")),
        P(None, ("row", "col")),
        P(("row", "col")),
        P("row", "col", None, None, None),
        P("row", "col", None, None),
        P("row", "col"),
    )
    return jax.shard_map(
        functools.partial(body, lay, total_len),
        mesh=mesh,
        in_specs=in_specs,
        out_specs=P(None, ("row", "col")),
        check_vma=False,
    )


def solution(mesh):
    return build(mesh, LAYOUT)
```

```python
import functools

import jax
import jax.numpy as jnp
from jax import lax
from jax.experimental import pallas as pl
from jax.experimental.pallas import tpu as pltpu
from jax.sharding import PartitionSpec as P

MESH = pl.DeviceIdType.MESH
HIGH = lax.Precision.HIGHEST
F32 = jnp.float32
BF16 = jnp.bfloat16

LAYOUT = dict(y_lo=4, z_far=4, y_hi=2, x=4, core=2)
NEAR = 4


class Place:
    def __init__(self, lay):
        self.lay = lay
        self.nz = lay["z_far"] * NEAR
        self.ncol = lay["y_hi"] * lay["x"] * lay["core"]
        self.fold = lay["x"] * lay["core"]
        self.ny = lay["y_lo"] * lay["y_hi"]
        self.r = lax.axis_index("row")
        self.c = lax.axis_index("col")
        self.y = lax.div(self.r, self.nz)
        self.z = lax.rem(self.r, self.nz)
        self.z_far = lax.div(self.z, NEAR)
        self.z_near = lax.rem(self.z, NEAR)
        self.y_hi = lax.div(self.c, self.fold)

    def row_at(self, dy, dz):
        y = lax.rem(self.y + dy, self.lay["y_lo"])
        z = lax.rem(self.z + dz, self.nz)
        return y * self.nz + z

    def at_z(self, dz):
        return (self.row_at(0, dz), self.c)

    def at_far(self, d, dy):
        return (self.row_at(dy, NEAR * d), self.c)

    def at_col(self, k):
        return (self.r, lax.rem(self.c + k, self.ncol))

    def at_fold(self, k):
        inner = lax.rem(self.c, self.fold)
        return (self.r, self.y_hi * self.fold + lax.rem(inner + k, self.fold))

    def at_y(self, k):
        y_lo = self.lay["y_lo"]
        y = lax.rem(self.y_hi * y_lo + self.y + k, self.ny)
        inner = lax.rem(self.c, self.fold)
        return (
            lax.rem(y, y_lo) * self.nz + self.z,
            lax.div(y, y_lo) * self.fold + inner,
        )

    def near_out(self):
        odd = lax.rem(self.z, 2)
        return (1, self.nz - 1, 2 + odd * (self.nz - 4))

    def near_in(self):
        odd = lax.rem(self.z, 2)
        return (self.nz - 1, 1, self.nz - 2 + odd * 4)


def split(values):
    high = values.astype(BF16)
    low = (values - high.astype(F32)).astype(BF16)
    return high, low


def apply_tile(vectors, weights):
    high, low = split(vectors)
    both = jnp.dot(jnp.concatenate([high, low], axis=0), weights, preferred_element_type=F32)
    width = weights.shape[1] // 2
    rows = vectors.shape[0]
    high_part = both[:rows, :width] + both[:rows, width:]
    return high_part + (both[rows:, :width] + both[rows:, width:])


def dot_nt(a, b):
    return lax.dot_general(
        a, b, (((1,), (1,)), ((), ())), precision=HIGH, preferred_element_type=F32
    )


def dot_nn(a, b):
    return jnp.dot(a, b, precision=HIGH, preferred_element_type=F32)


def normalise(gram, rows):
    count = gram.shape[0]
    tall = lax.broadcasted_iota(jnp.int32, (count, 1), 0)
    row_id = lax.broadcasted_iota(jnp.int32, rows.shape, 0)
    for j in range(count):
        inverse = lax.rsqrt(gram[j : j + 1, j : j + 1])
        column = jnp.where(tall > j, gram[:, j : j + 1] * inverse, 0.0)
        across = gram[j : j + 1, :] * inverse
        pivot = rows[j : j + 1, :] * inverse
        rows = jnp.where(row_id == j, jnp.broadcast_to(pivot, rows.shape), rows - column * pivot)
        gram = gram - column * across
    return rows


def kernel(
    lay,
    total_len,
    cur_hbm,
    prior_hbm,
    diag_hbm,
    tiles_hbm,
    where_ref,
    count_ref,
    out_ref,
    cur_ref,
    prior_ref,
    diag_ref,
    tiles,
    w_cols,
    w_rows,
    vec,
    far_in,
    col_in,
    terms,
    near_got,
    partial,
    far_got,
    col_terms,
    col_got,
    sums,
    fold_got,
    y_got,
    z_got,
    gb_sums,
    gb_fold,
    gb_y,
    gb_z,
    basis,
    cross,
    gmat,
    tile_sem,
    recv,
    gb_recv,
    sent,
    gb_sent,
):
    p = Place(lay)
    y_lo, z_far = lay["y_lo"], lay["z_far"]
    far = y_lo * z_far
    slots = tiles.shape[0]
    width = tiles.shape[1]
    k_rows = cur_ref.shape[0]

    fetches = [
        pltpu.make_async_copy(source, goal, tile_sem.at[i])
        for i, (source, goal) in enumerate(
            ((cur_hbm, cur_ref), (prior_hbm, prior_ref), (diag_hbm, diag_ref), (tiles_hbm, tiles))
        )
    ]
    for fetch in fetches:
        fetch.start()

    barrier = pltpu.get_barrier_semaphore()
    greet = [p.at_z(dz) for dz in range(1, p.nz)]
    greet += [p.at_far(d, dy) for d in range(z_far) for dy in range(1, y_lo)]
    greet += [p.at_col(k) for k in range(1, p.ncol)]
    for k in range(1, p.ny):
        if k != y_lo and lay["y_hi"] > 1:
            greet.append(p.at_y(k))
    for device in greet:
        pl.semaphore_signal(barrier, inc=1, device_id=device, device_id_type=MESH)

    n_basis = prior_ref.shape[0] + k_rows
    basis[...] = jnp.zeros(basis.shape, F32)
    cross[...] = jnp.zeros(cross.shape, F32)
    gmat[...] = jnp.zeros(gmat.shape, F32)
    fetches[0].wait()
    fetches[1].wait()
    basis[0, k_rows : n_basis] = prior_ref[...]
    basis[0, n_basis : n_basis + k_rows] = cur_ref[...]
    own = dot_nt(basis[0, k_rows : n_basis + k_rows], basis[0])
    packed = own[0:16] + pltpu.roll(own[16:32], 40, 1)
    packed = packed + jnp.concatenate(
        [pltpu.roll(own[32:40], 80, 1), jnp.zeros((8, width), F32)], axis=0
    )
    gb_sums[0] = packed
    vec[0] = cur_ref[...]
    far_in[0, 0, 0] = cur_ref[...]
    col_in[0, 0] = cur_ref[...]

    pl.semaphore_wait(barrier, len(greet))

    def send(src, dst, send_sem, recv_sem, device):
        pltpu.make_async_remote_copy(
            src_ref=src,
            dst_ref=dst,
            send_sem=send_sem,
            recv_sem=recv_sem,
            device_id=device,
            device_id_type=MESH,
        ).start()

    def wait_for(ref, sem):
        pltpu.make_async_copy(ref, ref, sem).wait()

    far_order = [d for d in (2, 1, 3) if d < z_far] + [0]
    near_order = [d for d in (0, 1, 3, 2) if d < z_far]

    def gather_start(s):
        for d in far_order:
            for dy in range(y_lo):
                if d or dy:
                    send(
                        vec.at[s],
                        far_in.at[s, 0, d * y_lo + dy],
                        sent.at[s, 0],
                        recv.at[s, d],
                        p.at_far(d, dy),
                    )
        for k in range(1, p.ncol):
            send(vec.at[s], col_in.at[s, k], sent.at[s, 1], recv.at[s, 4], p.at_col(k))

    def gather_rest(s):
        for d in near_order:
            first = 1 if d == 0 else 0
            arrived = far_in.at[s, 0, pl.ds(d * y_lo + first, y_lo - first)]
            wait_for(arrived, recv.at[s, d])
            chunk = pl.ds(d * y_lo, y_lo)
            for q, dz in enumerate(p.near_out()):
                send(
                    far_in.at[s, 0, chunk],
                    far_in.at[s, 1 + q, chunk],
                    sent.at[s, 2],
                    recv.at[s, 5],
                    p.at_z(dz),
                )
        wait_for(col_in.at[s, pl.ds(1, p.ncol - 1)], recv.at[s, 4])
        wait_for(far_in.at[s, pl.ds(1, 3)], recv.at[s, 5])

    def all_sum_stage(s, stage, value, got, ids, sem_s, sem_r, source):
        source[stage] = value
        for k, device in enumerate(ids):
            send(source.at[stage], got.at[k], sem_s, sem_r, device)

    def all_sum_wait(value, got, count, sem_r):
        wait_for(got, sem_r)
        total = value
        for k in range(count):
            total = total + got[k]
        return total

    fold_ids = [p.at_fold(k) for k in range(1, p.fold)]
    y_ids = [p.at_y(k) for k in range(1, p.ny)]
    z_ids = [p.at_z(k) for k in range(1, p.nz)]

    gather_start(0)
    for k, device in enumerate(fold_ids):
        send(gb_sums.at[0], gb_fold.at[k], gb_sent.at[0], gb_recv.at[0], device)

    fetches[2].wait()
    fetches[3].wait()
    count = count_ref[0, 0]

    def prepare(t, carry):
        tile = tiles[t]
        tile = jnp.where(t < count, tile, jnp.zeros_like(tile))
        high, low = split(tile)
        w_cols[t] = jnp.concatenate([high, low], axis=1)
        high, low = split(tile.T)
        w_rows[t] = jnp.concatenate([high, low], axis=1)
        return carry

    lax.fori_loop(0, slots, prepare, 0)

    near_out, near_in = p.near_out(), p.near_in()
    row_slot, far_slot, row_goal, far_goal = [], [], [], []
    for t in range(slots):
        at_row, at_col = where_ref[0, t], where_ref[1, t]
        row_slot.append(lax.rem(p.c - at_row + p.ncol, p.ncol))
        row_goal.append(lax.rem(at_row - p.c + p.ncol, p.ncol))
        y_t = lax.div(at_col, p.nz)
        z_t = lax.rem(at_col, p.nz)
        far_t = lax.div(z_t, NEAR)
        near_t = lax.rem(z_t, NEAR)
        slot = jnp.int32(0)
        goals = []
        dy_in = lax.rem(p.y - y_t + y_lo, y_lo)
        dy_out = lax.rem(y_t - p.y + y_lo, y_lo)
        for q in range(4):
            z_from = p.z if q == 0 else lax.rem(p.z + near_in[q - 1], p.nz)
            z_to = p.z if q == 0 else lax.rem(p.z + near_out[q - 1], p.nz)
            d_in = lax.rem(lax.div(z_from, NEAR) - far_t + z_far, z_far)
            here = q * far + d_in * y_lo + dy_in
            slot = jnp.where(lax.rem(z_from, NEAR) == near_t, here, slot)
            d_out = lax.rem(far_t - lax.div(z_to, NEAR) + z_far, z_far)
            there = d_out * y_lo + dy_out
            goals.append(jnp.where(lax.rem(z_to, NEAR) == near_t, there, -1))
        far_slot.append(slot)
        far_goal.append(goals)
    block_id = lax.broadcasted_iota(jnp.int32, (y_lo, k_rows, width), 0)
    col_id = lax.broadcasted_iota(jnp.int32, (p.ncol, k_rows, width), 0)

    def multiply(s):
        flat = far_in.at[s]
        to_cols = [apply_tile(col_in[s, row_slot[t]], w_cols[t]) for t in range(slots)]
        for d in far_order:
            for q in (1, 2, 3, 0):
                block = jnp.zeros(block_id.shape, F32)
                for t in range(slots):
                    hit = block_id == far_goal[t][q] - d * y_lo
                    block = block + jnp.where(hit, to_cols[t][None], 0.0)
                chunk = pl.ds(d * y_lo, y_lo)
                terms[s, q, chunk] = block
                if q:
                    send(
                        terms.at[s, q, chunk],
                        near_got.at[s, q - 1, chunk],
                        sent.at[s, 3],
                        recv.at[s, 6 + d],
                        p.at_z(near_out[q - 1]),
                    )
        block = jnp.zeros(col_id.shape, F32)
        for t in range(slots):
            q_t = lax.div(far_slot[t], far)
            to_rows = apply_tile(flat[q_t, lax.rem(far_slot[t], far)], w_rows[t])
            block = block + jnp.where(col_id == row_goal[t], to_rows[None], 0.0)
        col_terms[s] = block
        for k in range(1, p.ncol):
            send(col_terms.at[s, k], col_got.at[s, k - 1], sent.at[s, 4], recv.at[s, 10], p.at_col(k))

    def collect(s):
        for d in far_order:
            chunk = pl.ds(d * y_lo, y_lo)
            wait_for(near_got.at[s, pl.ds(0, 3), chunk], recv.at[s, 6 + d])
            total = terms[s, 0, chunk]
            for q in range(3):
                total = total + near_got[s, q, chunk]
            partial[s, chunk] = total
            for dy in range(y_lo):
                if d or dy:
                    at = d * y_lo + dy
                    send(partial.at[s, at], far_got.at[s, at - 1], sent.at[s, 5], recv.at[s, 11], p.at_far(d, dy))
        image = diag_ref[...] * vec[s] + col_terms[s, 0] + partial[s, 0]
        wait_for(col_got.at[s], recv.at[s, 10])
        for k in range(p.ncol - 1):
            image = image + col_got[s, k]
        wait_for(far_got.at[s], recv.at[s, 11])
        for k in range(far - 1):
            image = image + far_got[s, k]
        return image

    def gb_stage(value, stage, ids, got):
        gb_sums[stage] = value
        for k, device in enumerate(ids):
            send(gb_sums.at[stage], got.at[k], gb_sent.at[stage], gb_recv.at[stage], device)

    def gb_total(stage, got, n):
        wait_for(got, gb_recv.at[stage])
        total = gb_sums[stage]
        for k in range(n):
            total = total + got[k]
        return total

    lane = lax.broadcasted_iota(jnp.int32, (k_rows, width), 1)
    in_basis = (lane >= k_rows) & (lane < k_rows + n_basis)

    for s in range(2):
        if s:
            gather_start(s)
        gather_rest(s)
        multiply(s)
        if s == 0:
            gb_stage(gb_total(0, gb_fold, p.fold - 1), 1, y_ids, gb_y)
        image = collect(s)
        basis[s, 0:k_rows] = image
        value = dot_nt(image, basis[s])
        if s:
            value = value + dot_nt(vec[s], cross[...])
        all_sum_stage(s, 0, value, fold_got.at[s], fold_ids, sent.at[s, 6], recv.at[s, 12], sums.at[s])
        if s == 0:
            gb_stage(gb_total(1, gb_y, p.ny - 1), 2, z_ids, gb_z)
        value = all_sum_wait(value, fold_got.at[s], p.fold - 1, recv.at[s, 12])
        all_sum_stage(s, 1, value, y_got.at[s], y_ids, sent.at[s, 7], recv.at[s, 13], sums.at[s])
        value = all_sum_wait(value, y_got.at[s], p.ny - 1, recv.at[s, 13])
        all_sum_stage(s, 2, value, z_got.at[s], z_ids, sent.at[s, 8], recv.at[s, 14], sums.at[s])
        if s == 0:
            packed = gb_total(2, gb_z, p.nz - 1)
            wide = lax.broadcasted_iota(jnp.int32, packed.shape, 1)
            keep = (wide >= 8) & (wide < 48)
            gmat[0, 8:24] = jnp.where(keep, packed, 0.0)
            gmat[0, 24:40] = jnp.where(keep, pltpu.roll(packed, width - 40, 1), 0.0)
            gmat[0, 40:48] = jnp.where(keep, pltpu.roll(packed, width - 80, 1), 0.0)[0:8]
        value = all_sum_wait(value, z_got.at[s], p.nz - 1, recv.at[s, 14])

        inner = jnp.where(in_basis, value, 0.0)
        proj = inner * (1.0 / total_len)
        if s:
            newest = jnp.where(in_basis, pltpu.roll(value, width - 64, 1), 0.0)
            gmat[1, 40:48] = jnp.where(lane < 40, newest, 0.0)
            gmat[2, 40:48] = newest
            swept = dot_nn(proj, gmat[1]) + dot_nt(proj, gmat[2])
        else:
            swept = dot_nn(proj, gmat[0])
        gram = (value[:, 0:k_rows] + dot_nt(swept - 2.0 * inner, proj)) * (1.0 / total_len)
        remainder = image - dot_nn(proj, basis[s])
        fresh = normalise(gram, remainder)
        out_ref[s * k_rows : (s + 1) * k_rows] = fresh
        if s == 0:
            vec[1] = fresh
            far_in[1, 0, 0] = fresh
            col_in[1, 0] = fresh
            basis[1, 8:32] = prior_ref[8:32]
            basis[1, 32:40] = cur_ref[...]
            basis[1, 40:48] = fresh
            cross[72:112] = basis[1, 8:48]
            old = pltpu.roll(gmat[0, 16:48], width - 8, 1)
            wide = lax.broadcasted_iota(jnp.int32, old.shape, 1)
            gmat[1, 8:40] = jnp.where((wide >= 8) & (wide < 40), old, 0.0)

    for s in range(2):
        wait_for(far_in.at[s, 0, pl.ds(0, far - 1)], sent.at[s, 0])
        wait_for(col_in.at[s, pl.ds(1, p.ncol - 1)], sent.at[s, 1])
        wait_for(far_in.at[s, pl.ds(1, 3)], sent.at[s, 2])
        wait_for(near_got.at[s], sent.at[s, 3])
        wait_for(col_got.at[s], sent.at[s, 4])
        wait_for(far_got.at[s], sent.at[s, 5])
        wait_for(fold_got.at[s], sent.at[s, 6])
        wait_for(y_got.at[s], sent.at[s, 7])
        wait_for(z_got.at[s], sent.at[s, 8])
    wait_for(gb_fold, gb_sent.at[0])
    wait_for(gb_y, gb_sent.at[1])
    wait_for(gb_z, gb_sent.at[2])


def body(lay, total_len, current_block, prior_blocks, diagonal, stored_tiles, tile_coords, tile_counts):
    k_rows, width = current_block.shape
    slots = stored_tiles.shape[2]
    far = lay["y_lo"] * lay["z_far"]
    fold = lay["x"] * lay["core"]
    ncol = lay["y_hi"] * fold
    ny = lay["y_lo"] * lay["y_hi"]
    nz = lay["z_far"] * NEAR
    one = (k_rows, width)
    vmem = pl.BlockSpec(memory_space=pltpu.VMEM)
    smem = pl.BlockSpec(memory_space=pltpu.SMEM)
    anywhere = pl.BlockSpec(memory_space=pl.ANY)
    scratch = [
        pltpu.VMEM(one, F32),
        pltpu.VMEM((4 * k_rows, width), F32),
        pltpu.VMEM((1, width), F32),
        pltpu.VMEM((slots, width, width), F32),
        pltpu.VMEM((slots, width, 2 * width), BF16),
        pltpu.VMEM((slots, width, 2 * width), BF16),
        pltpu.VMEM((2, *one), F32),
        pltpu.VMEM((2, 4, far, *one), F32),
        pltpu.VMEM((2, ncol, *one), F32),
        pltpu.VMEM((2, 4, far, *one), F32),
        pltpu.VMEM((2, 3, far, *one), F32),
        pltpu.VMEM((2, far, *one), F32),
        pltpu.VMEM((2, far - 1, *one), F32),
        pltpu.VMEM((2, ncol, *one), F32),
        pltpu.VMEM((2, ncol - 1, *one), F32),
        pltpu.VMEM((2, 3, *one), F32),
        pltpu.VMEM((2, fold - 1, *one), F32),
        pltpu.VMEM((2, ny - 1, *one), F32),
        pltpu.VMEM((2, nz - 1, *one), F32),
        pltpu.VMEM((3, 2 * k_rows, width), F32),
        pltpu.VMEM((fold - 1, 2 * k_rows, width), F32),
        pltpu.VMEM((ny - 1, 2 * k_rows, width), F32),
        pltpu.VMEM((nz - 1, 2 * k_rows, width), F32),
        pltpu.VMEM((2, width, width), F32),
        pltpu.VMEM((width, width), F32),
        pltpu.VMEM((3, width, width), F32),
        pltpu.SemaphoreType.DMA((4,)),
        pltpu.SemaphoreType.DMA((2, 15)),
        pltpu.SemaphoreType.DMA((3,)),
        pltpu.SemaphoreType.DMA((2, 9)),
        pltpu.SemaphoreType.DMA((3,)),
    ]
    return pl.pallas_call(
        functools.partial(kernel, lay, total_len),
        out_shape=jax.ShapeDtypeStruct((2 * k_rows, width), F32),
        in_specs=[anywhere, anywhere, anywhere, anywhere, smem, smem],
        out_specs=vmem,
        scratch_shapes=scratch,
        compiler_params=pltpu.CompilerParams(
            collective_id=0, has_side_effects=True, vmem_limit_bytes=60 * 1024 * 1024
        ),
        name="lanczos",
    )(
        current_block,
        prior_blocks,
        diagonal[None, :],
        stored_tiles[0, 0],
        tile_coords[0, 0],
        tile_counts,
    )


def build(mesh, lay):
    total_len = float(128 * mesh.shape["row"] * mesh.shape["col"])
    in_specs = (
        P(None, ("row", "col")),
        P(None, ("row", "col")),
        P(("row", "col")),
        P("row", "col", None, None, None),
        P("row", "col", None, None),
        P("row", "col"),
    )
    return jax.shard_map(
        functools.partial(body, lay, total_len),
        mesh=mesh,
        in_specs=in_specs,
        out_specs=P(None, ("row", "col")),
        check_vma=False,
    )


def solution(mesh):
    return build(mesh, LAYOUT)
```
